32 devices in a mesh: section: 4 (over y, x), dp: 8 (over z, core).
Axes of the slice: x: 2, y: 2, z: 4, core: 2. Of those that a mesh axis runs over, the one named last changes fastest.
Arguments:
- latents: bfloat16 [4, 8, 4, 16, 8, 256], P(None, 'dp'), may hold values from -36 to 36
- cotangent: bfloat16 [4, 8, 4, 16, 8, 256], P(None, 'dp'), may hold values from -6 to 6
- spatial_kernels: bfloat16 [4, 2304, 256], P('section'), may hold values from -0.125 to 0.125
- temporal_kernels: bfloat16 [4, 768, 256], P('section'), may hold values from -0.21875 to 0.21875
Outputs:
- grad_spatial: float32 [4, 2304, 256], P('section', 'dp')
- grad_temporal: float32 [4, 768, 256], P('section', 'dp')
The draws below stay inside these ranges and needn't reach their ends.
All inputs are finite; a program needn't handle non-finite values.
Results may differ from the reference program's by a relative error of at most 0.017.
Values may be sent and summed in bfloat16 or wider, within the bound.
A program may use at most 128 MiB of HBM per device.

```python
import math
import jax
import jax.numpy as jnp
from jax import lax

C = 256
MICRO = 4
FR = 4
HT = 16
WD = 8
BATCH = 8
SECTIONS = 4


def draw_latents(key, part):
    shape = (MICRO, BATCH, FR, HT, WD, C)
    key_base, key_chan, key_cell = jax.random.split(key, 3)
    base = jnp.clip(jax.random.normal(key_base, shape, jnp.float32), -4.0, 4.0)
    low_end, high_end = (0.3, 3.0)
    chan_scale = jnp.exp(jax.random.uniform(key_chan, (C,), jnp.float32, math.log(low_end), math.log(high_end)))
    cell_scale = jnp.exp(jax.random.uniform(key_cell, shape[:-1] + (1,), jnp.float32, math.log(low_end), math.log(high_end)))
    return (base * chan_scale * cell_scale).astype(jnp.bfloat16)


def level_of(own_key, dims, pieces, low, top_value):
    def one(axis_at, parts):
        draws = jax.random.uniform(jax.random.fold_in(jax.random.fold_in(own_key, 6), axis_at), (parts,), jnp.float32, low / len(pieces), top_value / len(pieces))
        return jnp.repeat(jnp.exp(draws), dims[axis_at] // parts).reshape((-1,) + (1,) * (len(dims) - axis_at - 1))

    loudness = one(*pieces[0])
    for cut in pieces[1:]:
        loudness = loudness * one(*cut)
    return loudness


def centred(rng, extent, scale, limit, shards=(), held_as=jnp.bfloat16):
    entries = jax.random.normal(rng, extent, jnp.float32) * scale
    if len(shards) > 0:
        entries = level_of(rng, extent, shards, -0.22, 0.18) * entries
    return jnp.clip(entries, min=-limit, max=limit).astype(held_as)


def setup_inputs(seed: int = 0) -> dict:
    keys = jax.random.split(jax.random.key(seed), 5)
    latents = draw_latents(jax.random.fold_in(keys[4], 71), 0)
    cotangent = centred(keys[1], (MICRO, BATCH, FR, HT, WD, C), 1.0, 6.0, ((1, 8),))
    spatial_kernels = centred(keys[2], (SECTIONS, 9 * C, C), (9 * C) ** -0.5, 0.125, ((0, 4),))
    temporal_kernels = centred(keys[3], (SECTIONS, 3 * C, C), (3 * C) ** -0.5, 0.21875, ((0, 4),))
    return {"latents": latents, "cotangent": cotangent, "spatial_kernels": spatial_kernels, "temporal_kernels": temporal_kernels}


def silu_slope(value):
    sig = jax.nn.sigmoid(value)
    return sig * (1.0 + value * (1.0 - sig))

def flatten_cells(array):
    return array.reshape(-1, array.shape[-1])

def spatial_cols(source):
    height, width = (source.shape[2], source.shape[3])
    padded = jnp.pad(source, ((0, 0), (0, 0), (1, 1), (1, 1), (0, 0)))
    return jnp.concatenate([padded[:, :, row_tap:row_tap + height, col_tap:col_tap + width, :] for row_tap in range(3) for col_tap in range(3)], axis=-1)

def temporal_cols(source):
    frames = source.shape[1]
    padded = jnp.pad(source, ((0, 0), (2, 0), (0, 0), (0, 0), (0, 0)))
    return jnp.concatenate([padded[:, tap:tap + frames] for tap in range(3)], axis=-1)

def spatial_fold(columns, channels):
    height, width = (columns.shape[2], columns.shape[3])
    padded = jnp.pad(columns, ((0, 0), (0, 0), (1, 1), (1, 1), (0, 0)))
    total = jnp.zeros(columns.shape[:-1] + (channels,), jnp.float32)
    for row_tap in range(3):
        for col_tap in range(3):
            tap = row_tap * 3 + col_tap
            total = total + padded[:, :, 2 - row_tap:2 - row_tap + height, 2 - col_tap:2 - col_tap + width, tap * channels:(tap + 1) * channels]
    return total

def temporal_fold(columns, channels):
    frames = columns.shape[1]
    padded = jnp.pad(columns, ((0, 0), (0, 2), (0, 0), (0, 0), (0, 0)))
    total = jnp.zeros(columns.shape[:-1] + (channels,), jnp.float32)
    for tap in range(3):
        total = total + padded[:, 2 - tap:2 - tap + frames, :, :, tap * channels:(tap + 1) * channels]
    return total

def section_forward(section_in, w_spatial, w_temporal):
    act_f32 = section_in.astype(jnp.float32)
    inv_rms = lax.rsqrt(lax.optimization_barrier(jnp.mean(act_f32 * act_f32, axis=-1, keepdims=True)) + 1e-06)
    silu_one = jax.nn.silu(act_f32 * inv_rms).astype(jnp.bfloat16)
    cols_space = spatial_cols(silu_one)
    middle = jnp.dot(flatten_cells(cols_space), w_spatial, preferred_element_type=jnp.float32).reshape(section_in.shape)
    silu_two = jax.nn.silu(middle).astype(jnp.bfloat16)
    cols_time = temporal_cols(silu_two)
    branch = jnp.dot(flatten_cells(cols_time), w_temporal, preferred_element_type=jnp.float32).reshape(section_in.shape)
    return ((act_f32 + branch).astype(jnp.bfloat16), middle)

def section_backward(grad_out, section_in, middle, w_spatial, w_temporal):
    channels = section_in.shape[-1]
    act_f32 = section_in.astype(jnp.float32)
    inv_rms = lax.rsqrt(lax.optimization_barrier(jnp.mean(act_f32 * act_f32, axis=-1, keepdims=True)) + 1e-06)
    normed = act_f32 * inv_rms
    cols_space = spatial_cols(jax.nn.silu(normed).astype(jnp.bfloat16))
    cols_time = temporal_cols(jax.nn.silu(middle).astype(jnp.bfloat16))
    back_time = lax.dot_general(flatten_cells(grad_out), w_temporal, (((1,), (1,)), ((), ())), preferred_element_type=jnp.float32)
    time_back = temporal_fold(back_time.reshape(section_in.shape[:-1] + (3 * channels,)), channels)
    grad_mid = (time_back * silu_slope(middle)).astype(jnp.bfloat16)
    back_space = lax.dot_general(flatten_cells(grad_mid), w_spatial, (((1,), (1,)), ((), ())), preferred_element_type=jnp.float32)
    space_back = spatial_fold(back_space.reshape(section_in.shape[:-1] + (9 * channels,)), channels)
    grad_norm = space_back * silu_slope(normed)
    grad_act = inv_rms * grad_norm - act_f32 * (inv_rms * inv_rms * inv_rms) * lax.optimization_barrier(jnp.mean(grad_norm * act_f32, axis=-1, keepdims=True))
    grad_in = (grad_out.astype(jnp.float32) + grad_act).astype(jnp.bfloat16)
    return (cols_space, grad_mid, cols_time, grad_in)

def kernel_term(columns, grads):
    return lax.dot_general(flatten_cells(columns), flatten_cells(grads), (((0,), (0,)), ((), ())), preferred_element_type=jnp.float32)

def reference(latents, cotangent, spatial_kernels, temporal_kernels):
    section_count = spatial_kernels.shape[0]
    micro_count = latents.shape[0]
    sums_space = [jnp.zeros(spatial_kernels.shape[1:], jnp.float32) for _ in range(section_count)]
    sums_time = [jnp.zeros(temporal_kernels.shape[1:], jnp.float32) for _ in range(section_count)]
    for micro_idx in range(micro_count):
        current = latents[micro_idx]
        inputs = []
        middles = []
        for section_idx in range(section_count):
            inputs.append(current)
            current, middle = section_forward(current, spatial_kernels[section_idx], temporal_kernels[section_idx])
            middles.append(middle)
        grad_now = cotangent[micro_idx]
        for section_idx in range(section_count - 1, -1, -1):
            cols_space, grad_mid, cols_time, grad_in = section_backward(grad_now, inputs[section_idx], middles[section_idx], spatial_kernels[section_idx], temporal_kernels[section_idx])
            sums_space[section_idx] = sums_space[section_idx] + kernel_term(cols_space, grad_mid)
            sums_time[section_idx] = sums_time[section_idx] + kernel_term(cols_time, grad_now)
            grad_now = grad_in
    cells = latents.shape[0] * latents.shape[1] * latents.shape[2] * latents.shape[3] * latents.shape[4]
    grad_scale = 1.0 / math.sqrt(cells)
    return (grad_scale * jnp.stack(sums_space), grad_scale * jnp.stack(sums_time))
```

```python
import functools
import math

import jax
import jax.numpy as jnp
from jax import lax
from jax.experimental import pallas as pl
from jax.experimental.pallas import tpu as pltpu
from jax.sharding import PartitionSpec as P

MESH = pl.DeviceIdType.MESH
PER = 2


def slope_of(value, sig):
    return sig * (1.0 + value * (1.0 - sig))


def inv_rms_of(x):
    return lax.rsqrt(jnp.mean(x * x, axis=-1, keepdims=True) + 1e-06)


def column_shift(value, width, offset):
    cut = value.reshape(-1, width, value.shape[-1])
    col = lax.broadcasted_iota(jnp.int32, cut.shape, 1)
    rolled = pltpu.roll(cut, (-offset) % width, axis=1)
    edge = width - 1 if offset > 0 else 0
    return jnp.where(col == edge, 0.0, rolled).reshape(value.shape)


def dot(a, b):
    return jnp.dot(a, b, preferred_element_type=jnp.float32)


def kernel(
    dims,
    lat_ref, cot_ref, ws_ref, wt_ref,
    ds_ref, dt_ref,
    fwd_in, fwd_out, bwd_in, bwd_out,
    slope1, slope2, s1_t, s2_t, ws_t, wt_t,
    cols1, cols2, grads1, grads2, s2_prev, g_next, mixed, acc,
    f_send, f_recv, b_send, b_recv,
):
    micros, chunks, height, width, ch, sections = dims
    rows = height * PER * width
    line = PER * width
    total = micros * chunks
    sec = lax.axis_index("section")
    first = sec == 0
    last = sec == sections - 1

    barrier = pltpu.get_barrier_semaphore()

    @pl.when(jnp.logical_not(first))
    def _():
        pl.semaphore_signal(barrier, inc=1, device_id={"section": sec - 1}, device_id_type=MESH)

    @pl.when(jnp.logical_not(last))
    def _():
        pl.semaphore_signal(barrier, inc=1, device_id={"section": sec + 1}, device_id_type=MESH)

    acc[...] = jnp.zeros_like(acc)
    edge_rows = jnp.zeros((line, 3 * ch), jnp.bfloat16)
    cols1[0:line, :] = edge_rows
    cols1[line + rows : 2 * line + rows, :] = edge_rows
    for slot in range(chunks):
        grads1[slot, 0:line, :] = edge_rows
        grads1[slot, line + rows : 2 * line + rows, :] = edge_rows
    s2_prev[...] = jnp.zeros_like(s2_prev)
    g_next[...] = jnp.zeros_like(g_next)

    @pl.when(first | last)
    def _():
        pl.semaphore_wait(barrier, 1)

    @pl.when(jnp.logical_not(first | last))
    def _():
        pl.semaphore_wait(barrier, 2)

    def f_copy(k):
        return pltpu.make_async_remote_copy(
            src_ref=fwd_out.at[k], dst_ref=fwd_in.at[k],
            send_sem=f_send.at[k], recv_sem=f_recv.at[k],
            device_id={"section": sec + 1}, device_id_type=MESH,
        )

    def b_copy(k):
        return pltpu.make_async_remote_copy(
            src_ref=bwd_out.at[k], dst_ref=bwd_in.at[k],
            send_sem=b_send.at[k], recv_sem=b_recv.at[k],
            device_id={"section": sec - 1}, device_id_type=MESH,
        )

    def arrange(source, m, c, target, k):
        for f in range(PER):
            mixed[:, f] = source[m, c * PER + f].astype(jnp.float32)
        target[k] = mixed[...].reshape(rows, ch).astype(jnp.bfloat16)

    def forward(k):
        m, c = k // chunks, k % chunks

        @pl.when(first)
        def _():
            arrange(lat_ref, m, c, fwd_in, k)

        @pl.when(jnp.logical_not(first))
        def _():
            f_copy(k).wait_recv()

        x = fwd_in[k].astype(jnp.float32)
        u = x * inv_rms_of(x)
        sig = jax.nn.sigmoid(u)
        s1 = u * sig
        slope1[k] = slope_of(u, sig)
        s1b = s1.astype(jnp.bfloat16)
        cols1[line : line + rows, 0:ch] = column_shift(s1, width, -1).astype(jnp.bfloat16)
        cols1[line : line + rows, ch : 2 * ch] = s1b
        cols1[line : line + rows, 2 * ch : 3 * ch] = column_shift(s1, width, 1).astype(jnp.bfloat16)
        v = dot(cols1[0:rows, :], ws_ref[0 : 3 * ch, :])
        v += dot(cols1[line : line + rows, :], ws_ref[3 * ch : 6 * ch, :])
        v += dot(cols1[2 * line : 2 * line + rows, :], ws_ref[6 * ch : 9 * ch, :])
        sig2 = jax.nn.sigmoid(v)
        s2 = v * sig2
        slope2[k] = slope_of(v, sig2)
        s2b = s2.astype(jnp.bfloat16)

        @pl.when(jnp.logical_not(last))
        def _():
            now = s2.reshape(height, PER, width, ch)
            before = jnp.where(c == 0, 0.0, s2_prev[...])
            shifted = jnp.concatenate([before[:, 1:], now[:, :1]], axis=1)
            cols2[:, 0:ch] = before.reshape(rows, ch).astype(jnp.bfloat16)
            cols2[:, ch : 2 * ch] = shifted.reshape(rows, ch).astype(jnp.bfloat16)
            cols2[:, 2 * ch : 3 * ch] = s2b
            s2_prev[...] = now
            z = dot(cols2[...], wt_ref[...])
            fwd_out[k] = (x + z).astype(jnp.bfloat16)
            f_copy(k).start()

        s1_t[k] = s1b.T
        s2_t[k] = s2b.T

    def backward(j):
        m, c = j // chunks, chunks - 1 - j % chunks
        k = m * chunks + c

        @pl.when(last)
        def _():
            arrange(cot_ref, m, c, bwd_in, k)

        @pl.when(jnp.logical_not(last))
        def _():
            b_copy(k).wait_recv()

        gb = bwd_in[k]
        g = gb.astype(jnp.float32)
        now = g.reshape(height, PER, width, ch)
        after = jnp.where(c == chunks - 1, 0.0, g_next[...])
        shifted = jnp.concatenate([now[:, 1:], after[:, :1]], axis=1)
        grads2[c, :, 0:ch] = after.reshape(rows, ch).astype(jnp.bfloat16)
        grads2[c, :, ch : 2 * ch] = shifted.reshape(rows, ch).astype(jnp.bfloat16)
        grads2[c, :, 2 * ch : 3 * ch] = gb
        g_next[...] = now
        gmid = dot(grads2[c], wt_t[...]) * slope2[k]
        grads1[c, line : line + rows, 0:ch] = column_shift(gmid, width, 1).astype(jnp.bfloat16)
        grads1[c, line : line + rows, ch : 2 * ch] = gmid.astype(jnp.bfloat16)
        grads1[c, line : line + rows, 2 * ch : 3 * ch] = column_shift(gmid, width, -1).astype(jnp.bfloat16)

        @pl.when(jnp.logical_not(first))
        def _():
            back = dot(grads1[c, 2 * line : 2 * line + rows, :], ws_t[0 : 3 * ch, :])
            back += dot(grads1[c, line : line + rows, :], ws_t[3 * ch : 6 * ch, :])
            back += dot(grads1[c, 0:rows, :], ws_t[6 * ch : 9 * ch, :])
            gu = back * slope1[k]
            x = fwd_in[k].astype(jnp.float32)
            inv = inv_rms_of(x)
            gx = inv * gu - x * (inv * inv * inv) * jnp.mean(gu * x, axis=-1, keepdims=True)
            bwd_out[k] = (g + gx).astype(jnp.bfloat16)
            b_copy(k).start()

        @pl.when(c == 0)
        def _():
            for dr in range(3):
                top = (2 - dr) * line
                part = dot(s1_t[m * chunks], grads1[0, top : top + rows, :])
                for other in range(1, chunks):
                    part += dot(s1_t[m * chunks + other], grads1[other, top : top + rows, :])
                for dc in range(3):
                    acc[dr * 3 + dc] += part[:, dc * ch : (dc + 1) * ch]
            part = dot(s2_t[m * chunks], grads2[0])
            for other in range(1, chunks):
                part += dot(s2_t[m * chunks + other], grads2[other])
            for tap in range(3):
                acc[9 + tap] += part[:, tap * ch : (tap + 1) * ch]

    lag = chunks - 1 + 2 * (sections - 1)

    def tick(t, carry):
        i = t - sec

        @pl.when((i >= 0) & (i < total))
        def _():
            forward(i)

        @pl.when(t == jnp.where(first, sections - 1, 0))
        def _():
            for tap in range(9):
                ws_t[tap * ch : (tap + 1) * ch, :] = ws_ref[tap * ch : (tap + 1) * ch, :].T
            for tap in range(3):
                wt_t[tap * ch : (tap + 1) * ch, :] = wt_ref[tap * ch : (tap + 1) * ch, :].T

        j = t - (lag - sec)

        @pl.when((j >= 0) & (j < total))
        def _():
            backward(j)

        return carry

    lax.fori_loop(0, lag + total, tick, 0)

    for tap in range(9):
        ds_ref[tap * ch : (tap + 1) * ch, :] = acc[tap].astype(jnp.bfloat16)
    for tap in range(3):
        dt_ref[tap * ch : (tap + 1) * ch, :] = acc[9 + tap].astype(jnp.bfloat16)

    @pl.when(jnp.logical_not(last))
    def _():
        for k in range(total):
            f_copy(k).wait_send()

    @pl.when(jnp.logical_not(first))
    def _():
        for k in range(total):
            b_copy(k).wait_send()


def local(latents, cotangent, spatial_kernels, temporal_kernels):
    micros, crops, frames, height, width, ch = latents.shape
    sections = lax.axis_size("section")
    replicas = lax.axis_size("dp")
    chunks = frames // PER
    rows = height * PER * width
    line = PER * width
    total = micros * chunks
    vmem = pl.BlockSpec(memory_space=pltpu.VMEM)
    bf, f32 = jnp.bfloat16, jnp.float32
    hold_space, hold_time = pl.pallas_call(
        functools.partial(kernel, (micros, chunks, height, width, ch, sections)),
        out_shape=(
            jax.ShapeDtypeStruct((9 * ch, ch), bf),
            jax.ShapeDtypeStruct((3 * ch, ch), bf),
        ),
        in_specs=[vmem] * 4,
        out_specs=(vmem, vmem),
        scratch_shapes=[
            pltpu.VMEM((total, rows, ch), bf),
            pltpu.VMEM((total, rows, ch), bf),
            pltpu.VMEM((total, rows, ch), bf),
            pltpu.VMEM((total, rows, ch), bf),
            pltpu.VMEM((total, rows, ch), f32),
            pltpu.VMEM((total, rows, ch), f32),
            pltpu.VMEM((total, ch, rows), bf),
            pltpu.VMEM((total, ch, rows), bf),
            pltpu.VMEM((9 * ch, ch), bf),
            pltpu.VMEM((3 * ch, ch), bf),
            pltpu.VMEM((rows + 2 * line, 3 * ch), bf),
            pltpu.VMEM((rows, 3 * ch), bf),
            pltpu.VMEM((chunks, rows + 2 * line, 3 * ch), bf),
            pltpu.VMEM((chunks, rows, 3 * ch), bf),
            pltpu.VMEM((height, PER, width, ch), f32),
            pltpu.VMEM((height, PER, width, ch), f32),
            pltpu.VMEM((height, PER, width, ch), f32),
            pltpu.VMEM((12, ch, ch), f32),
            pltpu.SemaphoreType.DMA((total,)),
            pltpu.SemaphoreType.DMA((total,)),
            pltpu.SemaphoreType.DMA((total,)),
            pltpu.SemaphoreType.DMA((total,)),
        ],
        compiler_params=pltpu.CompilerParams(
            collective_id=0, has_side_effects=True, vmem_limit_bytes=48 * 1024 * 1024
        ),
    )(latents[:, 0], cotangent[:, 0], spatial_kernels[0], temporal_kernels[0])
    share_space = lax.psum_scatter(hold_space, "dp", scatter_dimension=0, tiled=True).astype(f32)
    share_time = lax.psum_scatter(hold_time, "dp", scatter_dimension=0, tiled=True).astype(f32)
    cells = micros * replicas * crops * frames * height * width
    grad_scale = 1.0 / math.sqrt(cells)
    return ((grad_scale * share_space)[None], (grad_scale * share_time)[None])


def solution(mesh):
    in_specs = (
        P(None, "dp", None, None, None, None),
        P(None, "dp", None, None, None, None),
        P("section", None, None),
        P("section", None, None),
    )
    out_specs = (P("section", "dp", None), P("section", "dp", None))
    return jax.shard_map(local, mesh=mesh, in_specs=in_specs, out_specs=out_specs, check_vma=False)
```

```python
import functools
import math

import jax
import jax.numpy as jnp
from jax import lax
from jax.experimental import pallas as pl
from jax.experimental.pallas import tpu as pltpu
from jax.sharding import PartitionSpec as P

MESH = pl.DeviceIdType.MESH
PER = 2


def slope_of(value, sig):
    return sig * (1.0 + value * (1.0 - sig))


def inv_rms_of(x):
    return lax.rsqrt(jnp.mean(x * x, axis=-1, keepdims=True) + 1e-06)


def column_shift(value, width, offset):
    cut = value.reshape(-1, width, value.shape[-1])
    col = lax.broadcasted_iota(jnp.int32, cut.shape, 1)
    rolled = pltpu.roll(cut, (-offset) % width, axis=1)
    edge = width - 1 if offset > 0 else 0
    return jnp.where(col == edge, 0.0, rolled).reshape(value.shape)


def dot(a, b):
    return jnp.dot(a, b, preferred_element_type=jnp.float32)


def kernel(
    dims,
    lat_hbm, cot_hbm, ws_hbm, wt_hbm,
    ds_ref, dt_ref,
    lat_ref, cot_ref, ws_ref, wt_ref,
    fwd_in, fwd_out, bwd_in, bwd_out,
    slope1, slope2, s1_t, s2_t, ws_t, wt_t,
    cols1, cols2, grads1, grads2, s2_prev, g_next, mixed, acc,
    pair_out, pair_in, chip_out, chip_in,
    load_sem, f_send, f_recv, b_send, b_recv,
    p_send, p_recv, c_send, c_recv,
):
    micros, chunks, height, width, ch, sections, replicas, grad_scale = dims
    rows = height * PER * width
    line = PER * width
    total = micros * chunks
    sec = lax.axis_index("section")
    first = sec == 0
    last = sec == sections - 1

    dp = lax.axis_index("dp")
    core, chip = dp % 2, dp // 2
    chips = replicas // 2
    n_space, n_time = 9 * ch // replicas, 3 * ch // replicas

    loads = [
        pltpu.make_async_copy(source, target, load_sem.at[at])
        for at, (source, target) in enumerate(
            ((ws_hbm, ws_ref), (wt_hbm, wt_ref), (lat_hbm, lat_ref), (cot_hbm, cot_ref))
        )
    ]

    @pl.when(first)
    def _():
        loads[2].start()

    loads[0].start()
    loads[1].start()

    @pl.when(last)
    def _():
        loads[3].start()

    barrier = pltpu.get_barrier_semaphore()
    pl.semaphore_signal(barrier, inc=1, device_id={"dp": dp + 1 - 2 * core}, device_id_type=MESH)
    for o in range(1, chips):
        peer = 2 * ((chip + o) % chips) + core
        pl.semaphore_signal(barrier, inc=1, device_id={"dp": peer}, device_id_type=MESH)

    @pl.when(jnp.logical_not(first))
    def _():
        pl.semaphore_signal(barrier, inc=1, device_id={"section": sec - 1}, device_id_type=MESH)

    @pl.when(jnp.logical_not(last))
    def _():
        pl.semaphore_signal(barrier, inc=1, device_id={"section": sec + 1}, device_id_type=MESH)

    acc[...] = jnp.zeros_like(acc)
    edge_rows = jnp.zeros((line, 3 * ch), jnp.bfloat16)
    cols1[0:line, :] = edge_rows
    cols1[line + rows : 2 * line + rows, :] = edge_rows
    for slot in range(chunks):
        grads1[slot, 0:line, :] = edge_rows
        grads1[slot, line + rows : 2 * line + rows, :] = edge_rows
    s2_prev[...] = jnp.zeros_like(s2_prev)
    g_next[...] = jnp.zeros_like(g_next)

    @pl.when(first | last)
    def _():
        pl.semaphore_wait(barrier, 1 + chips)

    @pl.when(jnp.logical_not(first | last))
    def _():
        pl.semaphore_wait(barrier, 2 + chips)

    @pl.when(first)
    def _():
        loads[2].wait()

    loads[0].wait()
    loads[1].wait()

    @pl.when(last)
    def _():
        loads[3].wait()

    def f_copy(k):
        return pltpu.make_async_remote_copy(
            src_ref=fwd_out.at[k], dst_ref=fwd_in.at[k],
            send_sem=f_send.at[k], recv_sem=f_recv.at[k],
            device_id={"section": sec + 1}, device_id_type=MESH,
        )

    def b_copy(k):
        return pltpu.make_async_remote_copy(
            src_ref=bwd_out.at[k], dst_ref=bwd_in.at[k],
            send_sem=b_send.at[k], recv_sem=b_recv.at[k],
            device_id={"section": sec - 1}, device_id_type=MESH,
        )

    def arrange(source, m, c, target, k):
        for f in range(PER):
            mixed[:, f] = source[m, c * PER + f].astype(jnp.float32)
        target[k] = mixed[...].reshape(rows, ch).astype(jnp.bfloat16)

    def forward(k):
        m, c = k // chunks, k % chunks

        @pl.when(first)
        def _():
            arrange(lat_ref, m, c, fwd_in, k)

        @pl.when(jnp.logical_not(first))
        def _():
            f_copy(k).wait_recv()

        x = fwd_in[k].astype(jnp.float32)
        u = x * inv_rms_of(x)
        sig = jax.nn.sigmoid(u)
        s1 = u * sig
        slope1[k] = slope_of(u, sig)
        s1b = s1.astype(jnp.bfloat16)
        cols1[line : line + rows, 0:ch] = column_shift(s1, width, -1).astype(jnp.bfloat16)
        cols1[line : line + rows, ch : 2 * ch] = s1b
        cols1[line : line + rows, 2 * ch : 3 * ch] = column_shift(s1, width, 1).astype(jnp.bfloat16)
        v = dot(cols1[0:rows, :], ws_ref[0 : 3 * ch, :])
        v += dot(cols1[line : line + rows, :], ws_ref[3 * ch : 6 * ch, :])
        v += dot(cols1[2 * line : 2 * line + rows, :], ws_ref[6 * ch : 9 * ch, :])
        sig2 = jax.nn.sigmoid(v)
        s2 = v * sig2
        slope2[k] = slope_of(v, sig2)
        s2b = s2.astype(jnp.bfloat16)

        @pl.when(jnp.logical_not(last))
        def _():
            now = s2.reshape(height, PER, width, ch)
            before = jnp.where(c == 0, 0.0, s2_prev[...])
            shifted = jnp.concatenate([before[:, 1:], now[:, :1]], axis=1)
            cols2[:, 0:ch] = before.reshape(rows, ch).astype(jnp.bfloat16)
            cols2[:, ch : 2 * ch] = shifted.reshape(rows, ch).astype(jnp.bfloat16)
            cols2[:, 2 * ch : 3 * ch] = s2b
            s2_prev[...] = now
            z = dot(cols2[...], wt_ref[...])
            fwd_out[k] = (x + z).astype(jnp.bfloat16)
            f_copy(k).start()

        s1_t[k] = s1b.T
        s2_t[k] = s2b.T

    def backward(j):
        m, c = j // chunks, chunks - 1 - j % chunks
        k = m * chunks + c

        @pl.when(last)
        def _():
            arrange(cot_ref, m, c, bwd_in, k)

        @pl.when(jnp.logical_not(last))
        def _():
            b_copy(k).wait_recv()

        gb = bwd_in[k]
        g = gb.astype(jnp.float32)
        now = g.reshape(height, PER, width, ch)
        after = jnp.where(c == chunks - 1, 0.0, g_next[...])
        shifted = jnp.concatenate([now[:, 1:], after[:, :1]], axis=1)
        grads2[c, :, 0:ch] = after.reshape(rows, ch).astype(jnp.bfloat16)
        grads2[c, :, ch : 2 * ch] = shifted.reshape(rows, ch).astype(jnp.bfloat16)
        grads2[c, :, 2 * ch : 3 * ch] = gb
        g_next[...] = now
        gmid = dot(grads2[c], wt_t[...]) * slope2[k]
        grads1[c, line : line + rows, 0:ch] = column_shift(gmid, width, 1).astype(jnp.bfloat16)
        grads1[c, line : line + rows, ch : 2 * ch] = gmid.astype(jnp.bfloat16)
        grads1[c, line : line + rows, 2 * ch : 3 * ch] = column_shift(gmid, width, -1).astype(jnp.bfloat16)

        @pl.when(jnp.logical_not(first))
        def _():
            back = dot(grads1[c, 2 * line : 2 * line + rows, :], ws_t[0 : 3 * ch, :])
            back += dot(grads1[c, line : line + rows, :], ws_t[3 * ch : 6 * ch, :])
            back += dot(grads1[c, 0:rows, :], ws_t[6 * ch : 9 * ch, :])
            gu = back * slope1[k]
            x = fwd_in[k].astype(jnp.float32)
            inv = inv_rms_of(x)
            gx = inv * gu - x * (inv * inv * inv) * jnp.mean(gu * x, axis=-1, keepdims=True)
            bwd_out[k] = (g + gx).astype(jnp.bfloat16)
            b_copy(k).start()

        @pl.when(c == 0)
        def _():
            for dr in range(3):
                top = (2 - dr) * line
                part = dot(s1_t[m * chunks], grads1[0, top : top + rows, :])
                for other in range(1, chunks):
                    part += dot(s1_t[m * chunks + other], grads1[other, top : top + rows, :])
                for dc in range(3):
                    acc[(dr * 3 + dc) * ch : (dr * 3 + dc + 1) * ch, :] += part[:, dc * ch : (dc + 1) * ch]
            part = dot(s2_t[m * chunks], grads2[0])
            for other in range(1, chunks):
                part += dot(s2_t[m * chunks + other], grads2[other])
            for tap in range(3):
                acc[(9 + tap) * ch : (10 + tap) * ch, :] += part[:, tap * ch : (tap + 1) * ch]

    lag = chunks - 1 + 2 * (sections - 1)

    def tick(t, carry):
        i = t - sec

        @pl.when((i >= 0) & (i < total))
        def _():
            forward(i)

        @pl.when(t == jnp.where(first, sections - 1, 0))
        def _():
            for tap in range(9):
                ws_t[tap * ch : (tap + 1) * ch, :] = ws_ref[tap * ch : (tap + 1) * ch, :].T
            for tap in range(3):
                wt_t[tap * ch : (tap + 1) * ch, :] = wt_ref[tap * ch : (tap + 1) * ch, :].T

        j = t - (lag - sec)

        @pl.when((j >= 0) & (j < total))
        def _():
            backward(j)

        return carry

    lax.fori_loop(0, lag + total, tick, 0)

    def piece(d):
        space = acc[pl.ds(pl.multiple_of(d * n_space, 8), n_space), :]
        time = acc[pl.ds(pl.multiple_of(9 * ch + d * n_time, 8), n_time), :]
        return jnp.concatenate([space, time], axis=0)

    def pair_copy(p):
        return pltpu.make_async_remote_copy(
            src_ref=pair_out.at[p], dst_ref=pair_in.at[p],
            send_sem=p_send.at[p], recv_sem=p_recv.at[p],
            device_id={"dp": dp + 1 - 2 * core}, device_id_type=MESH,
        )

    def chip_copy(p, slot):
        return pltpu.make_async_remote_copy(
            src_ref=chip_out.at[p], dst_ref=chip_in.at[slot],
            send_sem=c_send.at[p], recv_sem=c_recv.at[slot],
            device_id={"dp": 2 * p + core}, device_id_type=MESH,
        )

    order = [(chip + o) % chips for o in range(1, chips)]
    for p in order + [chip]:
        pair_out[p] = piece(2 * p + 1 - core).astype(jnp.bfloat16)
        pair_copy(p).start()
    for p in order:
        pair_copy(p).wait_recv()
        chip_out[p] = (piece(2 * p + core) + pair_in[p].astype(jnp.float32)).astype(jnp.bfloat16)
        chip_copy(p, chip).start()
    pair_copy(chip).wait_recv()
    share = piece(dp) + pair_in[chip].astype(jnp.float32)
    for p in order:
        chip_copy(p, p).wait_recv()
        share += chip_in[p].astype(jnp.float32)
    ds_ref[...] = grad_scale * share[:n_space]
    dt_ref[...] = grad_scale * share[n_space:]
    for p in order + [chip]:
        pair_copy(p).wait_send()
    for p in order:
        chip_copy(p, chip).wait_send()

    @pl.when(jnp.logical_not(last))
    def _():
        for k in range(total):
            f_copy(k).wait_send()

    @pl.when(jnp.logical_not(first))
    def _():
        for k in range(total):
            b_copy(k).wait_send()


def local(latents, cotangent, spatial_kernels, temporal_kernels):
    micros, crops, frames, height, width, ch = latents.shape
    sections = lax.axis_size("section")
    replicas = lax.axis_size("dp")
    chunks = frames // PER
    rows = height * PER * width
    line = PER * width
    total = micros * chunks
    vmem = pl.BlockSpec(memory_space=pltpu.VMEM)
    bf, f32 = jnp.bfloat16, jnp.float32
    chips = replicas // 2
    share = 12 * ch // replicas
    cells = micros * replicas * crops * frames * height * width
    grad_scale = 1.0 / math.sqrt(cells)
    grad_space, grad_time = pl.pallas_call(
        functools.partial(
            kernel, (micros, chunks, height, width, ch, sections, replicas, grad_scale)
        ),
        out_shape=(
            jax.ShapeDtypeStruct((9 * ch // replicas, ch), f32),
            jax.ShapeDtypeStruct((3 * ch // replicas, ch), f32),
        ),
        in_specs=[pl.BlockSpec(memory_space=pl.ANY)] * 4,
        out_specs=(vmem, vmem),
        scratch_shapes=[
            pltpu.VMEM((micros, frames, height, width, ch), bf),
            pltpu.VMEM((micros, frames, height, width, ch), bf),
            pltpu.VMEM((9 * ch, ch), bf),
            pltpu.VMEM((3 * ch, ch), bf),
            pltpu.VMEM((total, rows, ch), bf),
            pltpu.VMEM((total, rows, ch), bf),
            pltpu.VMEM((total, rows, ch), bf),
            pltpu.VMEM((total, rows, ch), bf),
            pltpu.VMEM((total, rows, ch), f32),
            pltpu.VMEM((total, rows, ch), f32),
            pltpu.VMEM((total, ch, rows), bf),
            pltpu.VMEM((total, ch, rows), bf),
            pltpu.VMEM((9 * ch, ch), bf),
            pltpu.VMEM((3 * ch, ch), bf),
            pltpu.VMEM((rows + 2 * line, 3 * ch), bf),
            pltpu.VMEM((rows, 3 * ch), bf),
            pltpu.VMEM((chunks, rows + 2 * line, 3 * ch), bf),
            pltpu.VMEM((chunks, rows, 3 * ch), bf),
            pltpu.VMEM((height, PER, width, ch), f32),
            pltpu.VMEM((height, PER, width, ch), f32),
            pltpu.VMEM((height, PER, width, ch), f32),
            pltpu.VMEM((12 * ch, ch), f32),
            pltpu.VMEM((chips, share, ch), bf),
            pltpu.VMEM((chips, share, ch), bf),
            pltpu.VMEM((chips, share, ch), bf),
            pltpu.VMEM((chips, share, ch), bf),
            pltpu.SemaphoreType.DMA((4,)),
            pltpu.SemaphoreType.DMA((total,)),
            pltpu.SemaphoreType.DMA((total,)),
            pltpu.SemaphoreType.DMA((total,)),
            pltpu.SemaphoreType.DMA((total,)),
            pltpu.SemaphoreType.DMA((chips,)),
            pltpu.SemaphoreType.DMA((chips,)),
            pltpu.SemaphoreType.DMA((chips,)),
            pltpu.SemaphoreType.DMA((chips,)),
        ],
        compiler_params=pltpu.CompilerParams(
            collective_id=0, has_side_effects=True, vmem_limit_bytes=48 * 1024 * 1024
        ),
    )(latents[:, 0], cotangent[:, 0], spatial_kernels[0], temporal_kernels[0])
    return (grad_space[None], grad_time[None])


def solution(mesh):
    in_specs = (
        P(None, "dp", None, None, None, None),
        P(None, "dp", None, None, None, None),
        P("section", None, None),
        P("section", None, None),
    )
    out_specs = (P("section", "dp", None), P("section", "dp", None))
    return jax.shard_map(local, mesh=mesh, in_specs=in_specs, out_specs=out_specs, check_vma=False)
```

```python
import functools
import math

import jax
import jax.numpy as jnp
from jax import lax
from jax.experimental import pallas as pl
from jax.experimental.pallas import tpu as pltpu
from jax.sharding import PartitionSpec as P

MESH = pl.DeviceIdType.MESH
PER = 2
CUT = 2


def slope_of(value, sig):
    return sig * (1.0 + value * (1.0 - sig))


def inv_rms_of(x):
    return lax.rsqrt(jnp.mean(x * x, axis=-1, keepdims=True) + 1e-06)


def column_shift(value, width, offset):
    cut = value.reshape(-1, width, value.shape[-1])
    col = lax.broadcasted_iota(jnp.int32, cut.shape, 1)
    rolled = pltpu.roll(cut, (-offset) % width, axis=1)
    edge = width - 1 if offset > 0 else 0
    return jnp.where(col == edge, 0.0, rolled).reshape(value.shape)


def dot(a, b):
    return jnp.dot(a, b, preferred_element_type=jnp.float32)


def kernel(
    dims,
    lat_hbm, cot_hbm, ws_hbm, wt_hbm,
    ds_ref, dt_ref,
    lat_ref, cot_ref, ws_ref, wt_ref,
    fwd_in, fwd_out, bwd_in, bwd_out,
    slope1, slope2, s1_t, s2_t, ws_t, wt_t,
    cols1, cols2, grads1, grads2, s2_prev, g_next, mixed, acc,
    pair_out, pair_in, chip_out, chip_in,
    load_sem, f_send, f_recv, b_send, b_recv,
    p_send, p_recv, c_send, c_recv,
):
    micros, chunks, height, width, ch, sections, replicas, grad_scale = dims
    rows = height * PER * width
    line = PER * width
    total = micros * chunks
    tall = height // CUT
    part_rows = rows // CUT
    sec = lax.axis_index("section")
    first = sec == 0
    last = sec == sections - 1

    dp = lax.axis_index("dp")
    core, chip = dp % 2, dp // 2
    chips = replicas // 2
    n_space, n_time = 9 * ch // replicas, 3 * ch // replicas

    loads = [
        pltpu.make_async_copy(source, target, load_sem.at[at])
        for at, (source, target) in enumerate(
            ((ws_hbm, ws_ref), (wt_hbm, wt_ref), (lat_hbm, lat_ref), (cot_hbm, cot_ref))
        )
    ]

    @pl.when(first)
    def _():
        loads[2].start()

    loads[0].start()
    loads[1].start()

    @pl.when(last)
    def _():
        loads[3].start()

    barrier = pltpu.get_barrier_semaphore()
    pl.semaphore_signal(barrier, inc=1, device_id={"dp": dp + 1 - 2 * core}, device_id_type=MESH)
    for o in range(1, chips):
        peer = 2 * ((chip + o) % chips) + core
        pl.semaphore_signal(barrier, inc=1, device_id={"dp": peer}, device_id_type=MESH)

    @pl.when(jnp.logical_not(first))
    def _():
        pl.semaphore_signal(barrier, inc=1, device_id={"section": sec - 1}, device_id_type=MESH)

    @pl.when(jnp.logical_not(last))
    def _():
        pl.semaphore_signal(barrier, inc=1, device_id={"section": sec + 1}, device_id_type=MESH)

    acc[...] = jnp.zeros_like(acc)
    edge_rows = jnp.zeros((line, 3 * ch), jnp.bfloat16)
    cols1[0:line, :] = edge_rows
    cols1[line + rows : 2 * line + rows, :] = edge_rows
    for slot in range(chunks):
        grads1[slot, 0:line, :] = edge_rows
        grads1[slot, line + rows : 2 * line + rows, :] = edge_rows
    s2_prev[...] = jnp.zeros_like(s2_prev)
    g_next[...] = jnp.zeros_like(g_next)

    @pl.when(first | last)
    def _():
        pl.semaphore_wait(barrier, 1 + chips)

    @pl.when(jnp.logical_not(first | last))
    def _():
        pl.semaphore_wait(barrier, 2 + chips)

    @pl.when(first)
    def _():
        loads[2].wait()

    loads[0].wait()
    loads[1].wait()

    @pl.when(last)
    def _():
        loads[3].wait()

    def f_copy(k):
        return pltpu.make_async_remote_copy(
            src_ref=fwd_out.at[k], dst_ref=fwd_in.at[k],
            send_sem=f_send.at[k], recv_sem=f_recv.at[k],
            device_id={"section": sec + 1}, device_id_type=MESH,
        )

    def b_copy(k):
        return pltpu.make_async_remote_copy(
            src_ref=bwd_out.at[k], dst_ref=bwd_in.at[k],
            send_sem=b_send.at[k], recv_sem=b_recv.at[k],
            device_id={"section": sec - 1}, device_id_type=MESH,
        )

    def arrange(source, m, c, target, k):
        for f in range(PER):
            mixed[:, f] = source[m, c * PER + f].astype(jnp.float32)
        for h in range(CUT):
            piece_in = mixed[h * tall : (h + 1) * tall].reshape(part_rows, ch)
            target[CUT * k + h] = piece_in.astype(jnp.bfloat16)

    def forward(k):
        m, c = k // chunks, k % chunks

        @pl.when(first)
        def _():
            arrange(lat_ref, m, c, fwd_in, k)

        s1_parts, s2_parts = [], []
        for h in range(CUT):
            q = CUT * k + h
            top = line + h * part_rows

            @pl.when(jnp.logical_not(first))
            def _():
                f_copy(q).wait_recv()

            x = fwd_in[q].astype(jnp.float32)
            u = x * inv_rms_of(x)
            sig = jax.nn.sigmoid(u)
            s1 = u * sig
            slope1[q] = slope_of(u, sig)
            s1b = s1.astype(jnp.bfloat16)
            s1_parts.append(s1b)
            left, right = column_shift(s1, width, -1), column_shift(s1, width, 1)
            cols1[top : top + part_rows, 0:ch] = left.astype(jnp.bfloat16)
            cols1[top : top + part_rows, ch : 2 * ch] = s1b
            cols1[top : top + part_rows, 2 * ch : 3 * ch] = right.astype(jnp.bfloat16)
        for h in range(CUT):
            q = CUT * k + h
            top = h * part_rows
            v = dot(cols1[top : top + part_rows, :], ws_ref[0 : 3 * ch, :])
            v += dot(cols1[top + line : top + line + part_rows, :], ws_ref[3 * ch : 6 * ch, :])
            v += dot(cols1[top + 2 * line : top + 2 * line + part_rows, :], ws_ref[6 * ch : 9 * ch, :])
            sig2 = jax.nn.sigmoid(v)
            s2 = v * sig2
            slope2[q] = slope_of(v, sig2)
            s2b = s2.astype(jnp.bfloat16)
            s2_parts.append(s2b)

            @pl.when(jnp.logical_not(last))
            def _():
                now = s2.reshape(tall, PER, width, ch)
                before = jnp.where(c == 0, 0.0, s2_prev[h * tall : (h + 1) * tall])
                shifted = jnp.concatenate([before[:, 1:], now[:, :1]], axis=1)
                cols2[top : top + part_rows, 0:ch] = before.reshape(part_rows, ch).astype(jnp.bfloat16)
                cols2[top : top + part_rows, ch : 2 * ch] = shifted.reshape(part_rows, ch).astype(jnp.bfloat16)
                cols2[top : top + part_rows, 2 * ch : 3 * ch] = s2b
                s2_prev[h * tall : (h + 1) * tall] = now
                z = dot(cols2[top : top + part_rows, :], wt_ref[...])
                fwd_out[q] = (fwd_in[q].astype(jnp.float32) + z).astype(jnp.bfloat16)
                f_copy(q).start()

        for h in range(CUT):
            s1_t[k, :, h * part_rows : (h + 1) * part_rows] = s1_parts[h].T
            s2_t[k, :, h * part_rows : (h + 1) * part_rows] = s2_parts[h].T

    def backward(j):
        m, c = j // chunks, chunks - 1 - j % chunks
        k = m * chunks + c

        @pl.when(last)
        def _():
            arrange(cot_ref, m, c, bwd_in, k)

        for h in range(CUT):
            q = CUT * k + h
            top = h * part_rows

            @pl.when(jnp.logical_not(last))
            def _():
                b_copy(q).wait_recv()

            gb = bwd_in[q]
            now = gb.astype(jnp.float32).reshape(tall, PER, width, ch)
            after = jnp.where(c == chunks - 1, 0.0, g_next[h * tall : (h + 1) * tall])
            shifted = jnp.concatenate([now[:, 1:], after[:, :1]], axis=1)
            grads2[c, top : top + part_rows, 0:ch] = after.reshape(part_rows, ch).astype(jnp.bfloat16)
            grads2[c, top : top + part_rows, ch : 2 * ch] = shifted.reshape(part_rows, ch).astype(jnp.bfloat16)
            grads2[c, top : top + part_rows, 2 * ch : 3 * ch] = gb
            g_next[h * tall : (h + 1) * tall] = now
            gmid = dot(grads2[c, top : top + part_rows, :], wt_t[...]) * slope2[q]
            top += line
            left, right = column_shift(gmid, width, 1), column_shift(gmid, width, -1)
            grads1[c, top : top + part_rows, 0:ch] = left.astype(jnp.bfloat16)
            grads1[c, top : top + part_rows, ch : 2 * ch] = gmid.astype(jnp.bfloat16)
            grads1[c, top : top + part_rows, 2 * ch : 3 * ch] = right.astype(jnp.bfloat16)

        @pl.when(jnp.logical_not(first))
        def _():
            for h in range(CUT):
                q = CUT * k + h
                top = h * part_rows
                back = dot(grads1[c, top + 2 * line : top + 2 * line + part_rows, :], ws_t[0 : 3 * ch, :])
                back += dot(grads1[c, top + line : top + line + part_rows, :], ws_t[3 * ch : 6 * ch, :])
                back += dot(grads1[c, top : top + part_rows, :], ws_t[6 * ch : 9 * ch, :])
                gu = back * slope1[q]
                x = fwd_in[q].astype(jnp.float32)
                inv = inv_rms_of(x)
                gx = inv * gu - x * (inv * inv * inv) * jnp.mean(gu * x, axis=-1, keepdims=True)
                bwd_out[q] = (bwd_in[q].astype(jnp.float32) + gx).astype(jnp.bfloat16)
                b_copy(q).start()

        @pl.when(c == 0)
        def _():
            for dr in range(3):
                top = (2 - dr) * line
                part = dot(s1_t[m * chunks], grads1[0, top : top + rows, :])
                for other in range(1, chunks):
                    part += dot(s1_t[m * chunks + other], grads1[other, top : top + rows, :])
                for dc in range(3):
                    acc[(dr * 3 + dc) * ch : (dr * 3 + dc + 1) * ch, :] += part[:, dc * ch : (dc + 1) * ch]
            part = dot(s2_t[m * chunks], grads2[0])
            for other in range(1, chunks):
                part += dot(s2_t[m * chunks + other], grads2[other])
            for tap in range(3):
                acc[(9 + tap) * ch : (10 + tap) * ch, :] += part[:, tap * ch : (tap + 1) * ch]

    lag = chunks - 1 + 2 * (sections - 1)

    def tick(t, carry):
        i = t - sec

        @pl.when((i >= 0) & (i < total))
        def _():
            forward(i)

        @pl.when(t == jnp.where(first, sections - 1, 0))
        def _():
            for tap in range(9):
                ws_t[tap * ch : (tap + 1) * ch, :] = ws_ref[tap * ch : (tap + 1) * ch, :].T
            for tap in range(3):
                wt_t[tap * ch : (tap + 1) * ch, :] = wt_ref[tap * ch : (tap + 1) * ch, :].T

        j = t - (lag - sec)

        @pl.when((j >= 0) & (j < total))
        def _():
            backward(j)

        return carry

    lax.fori_loop(0, lag + total, tick, 0)

    def piece(d):
        space = acc[pl.ds(pl.multiple_of(d * n_space, 8), n_space), :]
        time = acc[pl.ds(pl.multiple_of(9 * ch + d * n_time, 8), n_time), :]
        return jnp.concatenate([space, time], axis=0)

    def pair_copy(p):
        return pltpu.make_async_remote_copy(
            src_ref=pair_out.at[p], dst_ref=pair_in.at[p],
            send_sem=p_send.at[p], recv_sem=p_recv.at[p],
            device_id={"dp": dp + 1 - 2 * core}, device_id_type=MESH,
        )

    def chip_copy(p, slot):
        return pltpu.make_async_remote_copy(
            src_ref=chip_out.at[p], dst_ref=chip_in.at[slot],
            send_sem=c_send.at[p], recv_sem=c_recv.at[slot],
            device_id={"dp": 2 * p + core}, device_id_type=MESH,
        )

    order = [(chip + o) % chips for o in range(1, chips)]
    for p in order + [chip]:
        pair_out[p] = piece(2 * p + 1 - core).astype(jnp.bfloat16)
        pair_copy(p).start()
    for p in order:
        pair_copy(p).wait_recv()
        chip_out[p] = (piece(2 * p + core) + pair_in[p].astype(jnp.float32)).astype(jnp.bfloat16)
        chip_copy(p, chip).start()
    pair_copy(chip).wait_recv()
    share = piece(dp) + pair_in[chip].astype(jnp.float32)
    for p in order:
        chip_copy(p, p).wait_recv()
        share += chip_in[p].astype(jnp.float32)
    ds_ref[...] = grad_scale * share[:n_space]
    dt_ref[...] = grad_scale * share[n_space:]
    for p in order + [chip]:
        pair_copy(p).wait_send()
    for p in order:
        chip_copy(p, chip).wait_send()

    @pl.when(jnp.logical_not(last))
    def _():
        for k in range(CUT * total):
            f_copy(k).wait_send()

    @pl.when(jnp.logical_not(first))
    def _():
        for k in range(CUT * total):
            b_copy(k).wait_send()


def local(latents, cotangent, spatial_kernels, temporal_kernels):
    micros, crops, frames, height, width, ch = latents.shape
    sections = lax.axis_size("section")
    replicas = lax.axis_size("dp")
    chunks = frames // PER
    rows = height * PER * width
    line = PER * width
    total = micros * chunks
    vmem = pl.BlockSpec(memory_space=pltpu.VMEM)
    bf, f32 = jnp.bfloat16, jnp.float32
    chips = replicas // 2
    share = 12 * ch // replicas
    cells = micros * replicas * crops * frames * height * width
    grad_scale = 1.0 / math.sqrt(cells)
    grad_space, grad_time = pl.pallas_call(
        functools.partial(
            kernel, (micros, chunks, height, width, ch, sections, replicas, grad_scale)
        ),
        out_shape=(
            jax.ShapeDtypeStruct((9 * ch // replicas, ch), f32),
            jax.ShapeDtypeStruct((3 * ch // replicas, ch), f32),
        ),
        in_specs=[pl.BlockSpec(memory_space=pltpu.HBM)] * 4,
        out_specs=(vmem, vmem),
        scratch_shapes=[
            pltpu.VMEM((micros, frames, height, width, ch), bf),
            pltpu.VMEM((micros, frames, height, width, ch), bf),
            pltpu.VMEM((9 * ch, ch), bf),
            pltpu.VMEM((3 * ch, ch), bf),
            pltpu.VMEM((CUT * total, rows // CUT, ch), bf),
            pltpu.VMEM((CUT * total, rows // CUT, ch), bf),
            pltpu.VMEM((CUT * total, rows // CUT, ch), bf),
            pltpu.VMEM((CUT * total, rows // CUT, ch), bf),
            pltpu.VMEM((CUT * total, rows // CUT, ch), f32),
            pltpu.VMEM((CUT * total, rows // CUT, ch), f32),
            pltpu.VMEM((total, ch, rows), bf),
            pltpu.VMEM((total, ch, rows), bf),
            pltpu.VMEM((9 * ch, ch), bf),
            pltpu.VMEM((3 * ch, ch), bf),
            pltpu.VMEM((rows + 2 * line, 3 * ch), bf),
            pltpu.VMEM((rows, 3 * ch), bf),
            pltpu.VMEM((chunks, rows + 2 * line, 3 * ch), bf),
            pltpu.VMEM((chunks, rows, 3 * ch), bf),
            pltpu.VMEM((height, PER, width, ch), f32),
            pltpu.VMEM((height, PER, width, ch), f32),
            pltpu.VMEM((height, PER, width, ch), f32),
            pltpu.VMEM((12 * ch, ch), f32),
            pltpu.VMEM((chips, share, ch), bf),
            pltpu.VMEM((chips, share, ch), bf),
            pltpu.VMEM((chips, share, ch), bf),
            pltpu.VMEM((chips, share, ch), bf),
            pltpu.SemaphoreType.DMA((4,)),
            pltpu.SemaphoreType.DMA((CUT * total,)),
            pltpu.SemaphoreType.DMA((CUT * total,)),
            pltpu.SemaphoreType.DMA((CUT * total,)),
            pltpu.SemaphoreType.DMA((CUT * total,)),
            pltpu.SemaphoreType.DMA((chips,)),
            pltpu.SemaphoreType.DMA((chips,)),
            pltpu.SemaphoreType.DMA((chips,)),
            pltpu.SemaphoreType.DMA((chips,)),
        ],
        compiler_params=pltpu.CompilerParams(
            collective_id=0, has_side_effects=True, vmem_limit_bytes=48 * 1024 * 1024
        ),
    )(latents[:, 0], cotangent[:, 0], spatial_kernels[0], temporal_kernels[0])
    return (grad_space[None], grad_time[None])


def solution(mesh):
    in_specs = (
        P(None, "dp", None, None, None, None),
        P(None, "dp", None, None, None, None),
        P("section", None, None),
        P("section", None, None),
    )
    out_specs = (P("section", "dp", None), P("section", "dp", None))
    return jax.shard_map(local, mesh=mesh, in_specs=in_specs, out_specs=out_specs, check_vma=False)
```

```python
import functools
import math

import jax
import jax.numpy as jnp
from jax import lax
from jax.experimental import pallas as pl
from jax.experimental.pallas import tpu as pltpu
from jax.sharding import PartitionSpec as P

MESH = pl.DeviceIdType.MESH
PER = 2
CUT = 2


def slope_of(value, sig):
    return sig * (1.0 + value * (1.0 - sig))


def inv_rms_of(x):
    return lax.rsqrt(jnp.mean(x * x, axis=-1, keepdims=True) + 1e-06)


def column_shift(value, width, offset):
    cut = value.reshape(-1, width, value.shape[-1])
    col = lax.broadcasted_iota(jnp.int32, cut.shape, 1)
    rolled = pltpu.roll(cut, (-offset) % width, axis=1)
    edge = width - 1 if offset > 0 else 0
    return jnp.where(col == edge, 0.0, rolled).reshape(value.shape)


def dot(a, b):
    return jnp.dot(a, b, preferred_element_type=jnp.float32)


def kernel(
    dims,
    lat_hbm, cot_hbm, ws_hbm, wt_hbm,
    ds_ref, dt_ref,
    lat_ref, cot_ref, ws_ref, wt_ref,
    fwd_in, fwd_out, bwd_in, bwd_out,
    slope1, slope2, s1_t, s2_t, ws_t, wt_t,
    cols1, cols2, grads1, grads2, s2_prev, g_next, mixed, acc,
    pair_out, pair_in, chip_out, chip_in,
    load_sem, f_send, f_recv, b_send, b_recv,
    p_send, p_recv, c_send, c_recv,
):
    micros, chunks, height, width, ch, sections, replicas, grad_scale = dims
    rows = height * PER * width
    line = PER * width
    total = micros * chunks
    tall = height // CUT
    part_rows = rows // CUT
    sec = lax.axis_index("section")
    first = sec == 0
    last = sec == sections - 1

    dp = lax.axis_index("dp")
    core, chip = dp % 2, dp // 2
    chips = replicas // 2
    n_space, n_time = 9 * ch // replicas, 3 * ch // replicas

    loads = [
        pltpu.make_async_copy(source, target, load_sem.at[at])
        for at, (source, target) in enumerate(
            ((ws_hbm, ws_ref), (wt_hbm, wt_ref), (lat_hbm, lat_ref), (cot_hbm, cot_ref))
        )
    ]

    @pl.when(first)
    def _():
        loads[2].start()

    loads[0].start()
    loads[1].start()

    @pl.when(last)
    def _():
        loads[3].start()

    barrier = pltpu.get_barrier_semaphore()
    pl.semaphore_signal(barrier, inc=1, device_id={"dp": dp + 1 - 2 * core}, device_id_type=MESH)
    for o in range(1, chips):
        peer = 2 * ((chip + o) % chips) + core
        pl.semaphore_signal(barrier, inc=1, device_id={"dp": peer}, device_id_type=MESH)

    @pl.when(jnp.logical_not(first))
    def _():
        pl.semaphore_signal(barrier, inc=1, device_id={"section": sec - 1}, device_id_type=MESH)

    @pl.when(jnp.logical_not(last))
    def _():
        pl.semaphore_signal(barrier, inc=1, device_id={"section": sec + 1}, device_id_type=MESH)

    acc[...] = jnp.zeros_like(acc)
    edge_rows = jnp.zeros((line, 3 * ch), jnp.bfloat16)
    cols1[0:line, :] = edge_rows
    cols1[line + rows : 2 * line + rows, :] = edge_rows
    for slot in range(total):
        grads1[slot, 0:line, :] = edge_rows
        grads1[slot, line + rows : 2 * line + rows, :] = edge_rows
    s2_prev[...] = jnp.zeros_like(s2_prev)
    g_next[...] = jnp.zeros_like(g_next)

    @pl.when(first | last)
    def _():
        pl.semaphore_wait(barrier, 1 + chips)

    @pl.when(jnp.logical_not(first | last))
    def _():
        pl.semaphore_wait(barrier, 2 + chips)

    @pl.when(first)
    def _():
        loads[2].wait()

    loads[0].wait()
    loads[1].wait()

    @pl.when(last)
    def _():
        loads[3].wait()

    def f_copy(k):
        return pltpu.make_async_remote_copy(
            src_ref=fwd_out.at[k], dst_ref=fwd_in.at[k],
            send_sem=f_send.at[k], recv_sem=f_recv.at[k],
            device_id={"section": sec + 1}, device_id_type=MESH,
        )

    def b_copy(k):
        return pltpu.make_async_remote_copy(
            src_ref=bwd_out.at[k], dst_ref=bwd_in.at[k],
            send_sem=b_send.at[k], recv_sem=b_recv.at[k],
            device_id={"section": sec - 1}, device_id_type=MESH,
        )

    def arrange(source, m, c, target, k):
        for f in range(PER):
            mixed[:, f] = source[m, c * PER + f].astype(jnp.float32)
        for h in range(CUT):
            piece_in = mixed[h * tall : (h + 1) * tall].reshape(part_rows, ch)
            target[CUT * k + h] = piece_in.astype(jnp.bfloat16)

    def forward(k):
        m, c = k // chunks, k % chunks

        @pl.when(first)
        def _():
            arrange(lat_ref, m, c, fwd_in, k)

        s1_parts, s2_parts = [], []
        for h in range(CUT):
            q = CUT * k + h
            top = line + h * part_rows

            @pl.when(jnp.logical_not(first))
            def _():
                f_copy(q).wait_recv()

            x = fwd_in[q].astype(jnp.float32)
            u = x * inv_rms_of(x)
            sig = jax.nn.sigmoid(u)
            s1 = u * sig
            slope1[q] = slope_of(u, sig)
            s1b = s1.astype(jnp.bfloat16)
            s1_parts.append(s1b)
            left, right = column_shift(s1, width, -1), column_shift(s1, width, 1)
            cols1[top : top + part_rows, 0:ch] = left.astype(jnp.bfloat16)
            cols1[top : top + part_rows, ch : 2 * ch] = s1b
            cols1[top : top + part_rows, 2 * ch : 3 * ch] = right.astype(jnp.bfloat16)
        for h in range(CUT):
            q = CUT * k + h
            top = h * part_rows
            v = dot(cols1[top : top + part_rows, :], ws_ref[0 : 3 * ch, :])
            v += dot(cols1[top + line : top + line + part_rows, :], ws_ref[3 * ch : 6 * ch, :])
            v += dot(cols1[top + 2 * line : top + 2 * line + part_rows, :], ws_ref[6 * ch : 9 * ch, :])
            sig2 = jax.nn.sigmoid(v)
            s2 = v * sig2
            slope2[q] = slope_of(v, sig2)
            s2b = s2.astype(jnp.bfloat16)
            s2_parts.append(s2b)

            @pl.when(jnp.logical_not(last))
            def _():
                now = s2.reshape(tall, PER, width, ch)
                before = jnp.where(c == 0, 0.0, s2_prev[h * tall : (h + 1) * tall])
                shifted = jnp.concatenate([before[:, 1:], now[:, :1]], axis=1)
                cols2[top : top + part_rows, 0:ch] = before.reshape(part_rows, ch).astype(jnp.bfloat16)
                cols2[top : top + part_rows, ch : 2 * ch] = shifted.reshape(part_rows, ch).astype(jnp.bfloat16)
                cols2[top : top + part_rows, 2 * ch : 3 * ch] = s2b
                s2_prev[h * tall : (h + 1) * tall] = now
                z = dot(cols2[top : top + part_rows, :], wt_ref[...])
                fwd_out[q] = (fwd_in[q].astype(jnp.float32) + z).astype(jnp.bfloat16)
                f_copy(q).start()

        for h in range(CUT):
            s1_t[k, :, h * part_rows : (h + 1) * part_rows] = s1_parts[h].T
            s2_t[k, :, h * part_rows : (h + 1) * part_rows] = s2_parts[h].T

    def kernel_terms(m):
        spans = [m * chunks + c for c in range(chunks)]
        for dr in range(3):
            top = (2 - dr) * line
            part = sum(dot(s1_t[k], grads1[k, top : top + rows, :]) for k in spans)
            for dc in range(3):
                tap = dr * 3 + dc
                acc[tap * ch : (tap + 1) * ch, :] += part[:, dc * ch : (dc + 1) * ch]
        part = sum(dot(s2_t[k], grads2[k]) for k in spans)
        for tap in range(3):
            acc[(9 + tap) * ch : (10 + tap) * ch, :] += part[:, tap * ch : (tap + 1) * ch]

    def backward(j):
        m, c = j // chunks, chunks - 1 - j % chunks
        k = m * chunks + c

        @pl.when(last)
        def _():
            arrange(cot_ref, m, c, bwd_in, k)

        for h in range(CUT):
            q = CUT * k + h
            top = h * part_rows

            @pl.when(jnp.logical_not(last))
            def _():
                b_copy(q).wait_recv()

            gb = bwd_in[q]
            now = gb.astype(jnp.float32).reshape(tall, PER, width, ch)
            after = jnp.where(c == chunks - 1, 0.0, g_next[h * tall : (h + 1) * tall])
            shifted = jnp.concatenate([now[:, 1:], after[:, :1]], axis=1)
            grads2[k, top : top + part_rows, 0:ch] = after.reshape(part_rows, ch).astype(jnp.bfloat16)
            grads2[k, top : top + part_rows, ch : 2 * ch] = shifted.reshape(part_rows, ch).astype(jnp.bfloat16)
            grads2[k, top : top + part_rows, 2 * ch : 3 * ch] = gb
            g_next[h * tall : (h + 1) * tall] = now
            gmid = dot(grads2[k, top : top + part_rows, :], wt_t[...]) * slope2[q]
            top += line
            left, right = column_shift(gmid, width, 1), column_shift(gmid, width, -1)
            grads1[k, top : top + part_rows, 0:ch] = left.astype(jnp.bfloat16)
            grads1[k, top : top + part_rows, ch : 2 * ch] = gmid.astype(jnp.bfloat16)
            grads1[k, top : top + part_rows, 2 * ch : 3 * ch] = right.astype(jnp.bfloat16)

        @pl.when(jnp.logical_not(first))
        def _():
            for h in range(CUT):
                q = CUT * k + h
                top = h * part_rows
                back = dot(grads1[k, top + 2 * line : top + 2 * line + part_rows, :], ws_t[0 : 3 * ch, :])
                back += dot(grads1[k, top + line : top + line + part_rows, :], ws_t[3 * ch : 6 * ch, :])
                back += dot(grads1[k, top : top + part_rows, :], ws_t[6 * ch : 9 * ch, :])
                gu = back * slope1[q]
                x = fwd_in[q].astype(jnp.float32)
                inv = inv_rms_of(x)
                gx = inv * gu - x * (inv * inv * inv) * jnp.mean(gu * x, axis=-1, keepdims=True)
                bwd_out[q] = (bwd_in[q].astype(jnp.float32) + gx).astype(jnp.bfloat16)
                b_copy(q).start()

        @pl.when(first & (c == 0))
        def _():
            kernel_terms(m)

    lag = chunks - 1 + 2 * (sections - 1)

    def tick(t, carry):
        i = t - sec

        @pl.when((i >= 0) & (i < total))
        def _():
            forward(i)

        @pl.when(t == jnp.where(first, sections - 1, 0))
        def _():
            for tap in range(9):
                ws_t[tap * ch : (tap + 1) * ch, :] = ws_ref[tap * ch : (tap + 1) * ch, :].T
            for tap in range(3):
                wt_t[tap * ch : (tap + 1) * ch, :] = wt_ref[tap * ch : (tap + 1) * ch, :].T

        j = t - (lag - sec)

        @pl.when((j >= 0) & (j < total))
        def _():
            backward(j)

        return carry

    lax.fori_loop(0, lag + total, tick, 0)

    @pl.when(jnp.logical_not(first))
    def _():
        def late(m, carry):
            kernel_terms(m)
            return carry

        lax.fori_loop(0, micros, late, 0)

    def piece(d):
        space = acc[pl.ds(pl.multiple_of(d * n_space, 8), n_space), :]
        time = acc[pl.ds(pl.multiple_of(9 * ch + d * n_time, 8), n_time), :]
        return jnp.concatenate([space, time], axis=0)

    def pair_copy(p):
        return pltpu.make_async_remote_copy(
            src_ref=pair_out.at[p], dst_ref=pair_in.at[p],
            send_sem=p_send.at[p], recv_sem=p_recv.at[p],
            device_id={"dp": dp + 1 - 2 * core}, device_id_type=MESH,
        )

    def chip_copy(p, slot):
        return pltpu.make_async_remote_copy(
            src_ref=chip_out.at[p], dst_ref=chip_in.at[slot],
            send_sem=c_send.at[p], recv_sem=c_recv.at[slot],
            device_id={"dp": 2 * p + core}, device_id_type=MESH,
        )

    order = [(chip + o) % chips for o in range(1, chips)]
    for p in order + [chip]:
        pair_out[p] = piece(2 * p + 1 - core).astype(jnp.bfloat16)
        pair_copy(p).start()
    for p in order:
        pair_copy(p).wait_recv()
        chip_out[p] = (piece(2 * p + core) + pair_in[p].astype(jnp.float32)).astype(jnp.bfloat16)
        chip_copy(p, chip).start()
    pair_copy(chip).wait_recv()
    share = piece(dp) + pair_in[chip].astype(jnp.float32)
    for p in order:
        chip_copy(p, p).wait_recv()
        share += chip_in[p].astype(jnp.float32)
    ds_ref[...] = grad_scale * share[:n_space]
    dt_ref[...] = grad_scale * share[n_space:]
    for p in order + [chip]:
        pair_copy(p).wait_send()
    for p in order:
        chip_copy(p, chip).wait_send()

    @pl.when(jnp.logical_not(last))
    def _():
        for k in range(CUT * total):
            f_copy(k).wait_send()

    @pl.when(jnp.logical_not(first))
    def _():
        for k in range(CUT * total):
            b_copy(k).wait_send()


def local(latents, cotangent, spatial_kernels, temporal_kernels):
    micros, crops, frames, height, width, ch = latents.shape
    sections = lax.axis_size("section")
    replicas = lax.axis_size("dp")
    chunks = frames // PER
    rows = height * PER * width
    line = PER * width
    total = micros * chunks
    vmem = pl.BlockSpec(memory_space=pltpu.VMEM)
    bf, f32 = jnp.bfloat16, jnp.float32
    chips = replicas // 2
    share = 12 * ch // replicas
    cells = micros * replicas * crops * frames * height * width
    grad_scale = 1.0 / math.sqrt(cells)
    grad_space, grad_time = pl.pallas_call(
        functools.partial(
            kernel, (micros, chunks, height, width, ch, sections, replicas, grad_scale)
        ),
        out_shape=(
            jax.ShapeDtypeStruct((9 * ch // replicas, ch), f32),
            jax.ShapeDtypeStruct((3 * ch // replicas, ch), f32),
        ),
        in_specs=[pl.BlockSpec(memory_space=pltpu.HBM)] * 4,
        out_specs=(vmem, vmem),
        scratch_shapes=[
            pltpu.VMEM((micros, frames, height, width, ch), bf),
            pltpu.VMEM((micros, frames, height, width, ch), bf),
            pltpu.VMEM((9 * ch, ch), bf),
            pltpu.VMEM((3 * ch, ch), bf),
            pltpu.VMEM((CUT * total, rows // CUT, ch), bf),
            pltpu.VMEM((CUT * total, rows // CUT, ch), bf),
            pltpu.VMEM((CUT * total, rows // CUT, ch), bf),
            pltpu.VMEM((CUT * total, rows // CUT, ch), bf),
            pltpu.VMEM((CUT * total, rows // CUT, ch), f32),
            pltpu.VMEM((CUT * total, rows // CUT, ch), f32),
            pltpu.VMEM((total, ch, rows), bf),
            pltpu.VMEM((total, ch, rows), bf),
            pltpu.VMEM((9 * ch, ch), bf),
            pltpu.VMEM((3 * ch, ch), bf),
            pltpu.VMEM((rows + 2 * line, 3 * ch), bf),
            pltpu.VMEM((rows, 3 * ch), bf),
            pltpu.VMEM((total, rows + 2 * line, 3 * ch), bf),
            pltpu.VMEM((total, rows, 3 * ch), bf),
            pltpu.VMEM((height, PER, width, ch), f32),
            pltpu.VMEM((height, PER, width, ch), f32),
            pltpu.VMEM((height, PER, width, ch), f32),
            pltpu.VMEM((12 * ch, ch), f32),
            pltpu.VMEM((chips, share, ch), bf),
            pltpu.VMEM((chips, share, ch), bf),
            pltpu.VMEM((chips, share, ch), bf),
            pltpu.VMEM((chips, share, ch), bf),
            pltpu.SemaphoreType.DMA((4,)),
            pltpu.SemaphoreType.DMA((CUT * total,)),
            pltpu.SemaphoreType.DMA((CUT * total,)),
            pltpu.SemaphoreType.DMA((CUT * total,)),
            pltpu.SemaphoreType.DMA((CUT * total,)),
            pltpu.SemaphoreType.DMA((chips,)),
            pltpu.SemaphoreType.DMA((chips,)),
            pltpu.SemaphoreType.DMA((chips,)),
            pltpu.SemaphoreType.DMA((chips,)),
        ],
        compiler_params=pltpu.CompilerParams(
            collective_id=0, has_side_effects=True, vmem_limit_bytes=62 * 1024 * 1024
        ),
    )(latents[:, 0], cotangent[:, 0], spatial_kernels[0], temporal_kernels[0])
    return (grad_space[None], grad_time[None])


def solution(mesh):
    in_specs = (
        P(None, "dp", None, None, None, None),
        P(None, "dp", None, None, None, None),
        P("section", None, None),
        P("section", None, None),
    )
    out_specs = (P("section", "dp", None), P("section", "dp", None))
    return jax.shard_map(local, mesh=mesh, in_specs=in_specs, out_specs=out_specs, check_vma=False)
```

```python
import functools
import math

import jax
import jax.numpy as jnp
from jax import lax
from jax.experimental import pallas as pl
from jax.experimental.pallas import tpu as pltpu
from jax.sharding import PartitionSpec as P

MESH = pl.DeviceIdType.MESH
PER = 2
CUT = 1


def slope_of(value, sig):
    return sig * (1.0 + value * (1.0 - sig))


def inv_rms_of(x):
    return lax.rsqrt(jnp.mean(x * x, axis=-1, keepdims=True) + 1e-06)


def column_shift(value, width, offset):
    cut = value.reshape(-1, width, value.shape[-1])
    col = lax.broadcasted_iota(jnp.int32, cut.shape, 1)
    rolled = pltpu.roll(cut, (-offset) % width, axis=1)
    edge = width - 1 if offset > 0 else 0
    return jnp.where(col == edge, 0.0, rolled).reshape(value.shape)


def dot(a, b):
    return jnp.dot(a, b, preferred_element_type=jnp.float32)


def kernel(
    dims,
    lat_hbm, cot_hbm, ws_hbm, wt_hbm,
    ds_ref, dt_ref,
    lat_ref, cot_ref, ws_ref, wt_ref,
    fwd_in, fwd_out, bwd_in, bwd_out,
    slope1, slope2, s1_t, s2_t, ws_t, wt_t,
    cols1, cols2, grads1, grads2, s2_prev, g_next, mixed, acc,
    pair_out, pair_in, chip_out, chip_in,
    load_sem, f_send, f_recv, b_send, b_recv,
    p_send, p_recv, c_send, c_recv,
):
    micros, chunks, height, width, ch, sections, replicas, grad_scale = dims
    rows = height * PER * width
    line = PER * width
    total = micros * chunks
    tall = height // CUT
    part_rows = rows // CUT
    sec = lax.axis_index("section")
    first = sec == 0
    last = sec == sections - 1

    dp = lax.axis_index("dp")
    core, chip = dp % 2, dp // 2
    chips = replicas // 2
    n_space, n_time = 9 * ch // replicas, 3 * ch // replicas

    loads = [
        pltpu.make_async_copy(source, target, load_sem.at[at])
        for at, (source, target) in enumerate(
            ((ws_hbm, ws_ref), (wt_hbm, wt_ref), (lat_hbm, lat_ref), (cot_hbm, cot_ref))
        )
    ]

    @pl.when(first)
    def _():
        loads[2].start()

    loads[0].start()
    loads[1].start()

    @pl.when(last)
    def _():
        loads[3].start()

    barrier = pltpu.get_barrier_semaphore()
    pl.semaphore_signal(barrier, inc=1, device_id={"dp": dp + 1 - 2 * core}, device_id_type=MESH)
    for o in range(1, chips):
        peer = 2 * ((chip + o) % chips) + core
        pl.semaphore_signal(barrier, inc=1, device_id={"dp": peer}, device_id_type=MESH)

    @pl.when(jnp.logical_not(first))
    def _():
        pl.semaphore_signal(barrier, inc=1, device_id={"section": sec - 1}, device_id_type=MESH)

    @pl.when(jnp.logical_not(last))
    def _():
        pl.semaphore_signal(barrier, inc=1, device_id={"section": sec + 1}, device_id_type=MESH)

    acc[...] = jnp.zeros_like(acc)
    edge_rows = jnp.zeros((line, 3 * ch), jnp.bfloat16)
    cols1[0:line, :] = edge_rows
    cols1[line + rows : 2 * line + rows, :] = edge_rows
    for slot in range(total):
        grads1[slot, 0:line, :] = edge_rows
        grads1[slot, line + rows : 2 * line + rows, :] = edge_rows
    s2_prev[...] = jnp.zeros_like(s2_prev)
    g_next[...] = jnp.zeros_like(g_next)

    @pl.when(first | last)
    def _():
        pl.semaphore_wait(barrier, 1 + chips)

    @pl.when(jnp.logical_not(first | last))
    def _():
        pl.semaphore_wait(barrier, 2 + chips)

    @pl.when(first)
    def _():
        loads[2].wait()

    loads[0].wait()
    loads[1].wait()

    @pl.when(last)
    def _():
        loads[3].wait()

    def f_copy(k):
        return pltpu.make_async_remote_copy(
            src_ref=fwd_out.at[k], dst_ref=fwd_in.at[k],
            send_sem=f_send.at[k], recv_sem=f_recv.at[k],
            device_id={"section": sec + 1}, device_id_type=MESH,
        )

    def b_copy(k):
        return pltpu.make_async_remote_copy(
            src_ref=bwd_out.at[k], dst_ref=bwd_in.at[k],
            send_sem=b_send.at[k], recv_sem=b_recv.at[k],
            device_id={"section": sec - 1}, device_id_type=MESH,
        )

    def arrange(source, m, c, target, k):
        for f in range(PER):
            mixed[:, f] = source[m, c * PER + f].astype(jnp.float32)
        for h in range(CUT):
            piece_in = mixed[h * tall : (h + 1) * tall].reshape(part_rows, ch)
            target[CUT * k + h] = piece_in.astype(jnp.bfloat16)

    def forward(k):
        m, c = k // chunks, k % chunks

        @pl.when(first)
        def _():
            arrange(lat_ref, m, c, fwd_in, k)

        s1_parts, s2_parts = [], []
        for h in range(CUT):
            q = CUT * k + h
            top = line + h * part_rows

            @pl.when(jnp.logical_not(first))
            def _():
                f_copy(q).wait_recv()

            x = fwd_in[q].astype(jnp.float32)
            u = x * inv_rms_of(x)
            sig = jax.nn.sigmoid(u)
            s1 = u * sig
            slope1[q] = slope_of(u, sig)
            s1b = s1.astype(jnp.bfloat16)
            s1_parts.append(s1b)
            left, right = column_shift(s1, width, -1), column_shift(s1, width, 1)
            cols1[top : top + part_rows, 0:ch] = left.astype(jnp.bfloat16)
            cols1[top : top + part_rows, ch : 2 * ch] = s1b
            cols1[top : top + part_rows, 2 * ch : 3 * ch] = right.astype(jnp.bfloat16)
        for h in range(CUT):
            q = CUT * k + h
            top = h * part_rows
            v = dot(cols1[top : top + part_rows, :], ws_ref[0 : 3 * ch, :])
            v += dot(cols1[top + line : top + line + part_rows, :], ws_ref[3 * ch : 6 * ch, :])
            v += dot(cols1[top + 2 * line : top + 2 * line + part_rows, :], ws_ref[6 * ch : 9 * ch, :])
            sig2 = jax.nn.sigmoid(v)
            s2 = v * sig2
            slope2[q] = slope_of(v, sig2)
            s2b = s2.astype(jnp.bfloat16)
            s2_parts.append(s2b)

            @pl.when(jnp.logical_not(last))
            def _():
                now = s2.reshape(tall, PER, width, ch)
                before = jnp.where(c == 0, 0.0, s2_prev[h * tall : (h + 1) * tall])
                shifted = jnp.concatenate([before[:, 1:], now[:, :1]], axis=1)
                cols2[top : top + part_rows, 0:ch] = before.reshape(part_rows, ch).astype(jnp.bfloat16)
                cols2[top : top + part_rows, ch : 2 * ch] = shifted.reshape(part_rows, ch).astype(jnp.bfloat16)
                cols2[top : top + part_rows, 2 * ch : 3 * ch] = s2b
                s2_prev[h * tall : (h + 1) * tall] = now
                z = dot(cols2[top : top + part_rows, :], wt_ref[...])
                fwd_out[q] = (fwd_in[q].astype(jnp.float32) + z).astype(jnp.bfloat16)
                f_copy(q).start()

        for h in range(CUT):
            s1_t[k, :, h * part_rows : (h + 1) * part_rows] = s1_parts[h].T
            s2_t[k, :, h * part_rows : (h + 1) * part_rows] = s2_parts[h].T

    def kernel_terms(m):
        spans = [m * chunks + c for c in range(chunks)]
        for dr in range(3):
            top = (2 - dr) * line
            part = sum(dot(s1_t[k], grads1[k, top : top + rows, :]) for k in spans)
            for dc in range(3):
                tap = dr * 3 + dc
                acc[tap * ch : (tap + 1) * ch, :] += part[:, dc * ch : (dc + 1) * ch]
        part = sum(dot(s2_t[k], grads2[k]) for k in spans)
        for tap in range(3):
            acc[(9 + tap) * ch : (10 + tap) * ch, :] += part[:, tap * ch : (tap + 1) * ch]

    def backward(j):
        m, c = j // chunks, chunks - 1 - j % chunks
        k = m * chunks + c

        @pl.when(last)
        def _():
            arrange(cot_ref, m, c, bwd_in, k)

        for h in range(CUT):
            q = CUT * k + h
            top = h * part_rows

            @pl.when(jnp.logical_not(last))
            def _():
                b_copy(q).wait_recv()

            gb = bwd_in[q]
            now = gb.astype(jnp.float32).reshape(tall, PER, width, ch)
            after = jnp.where(c == chunks - 1, 0.0, g_next[h * tall : (h + 1) * tall])
            shifted = jnp.concatenate([now[:, 1:], after[:, :1]], axis=1)
            grads2[k, top : top + part_rows, 0:ch] = after.reshape(part_rows, ch).astype(jnp.bfloat16)
            grads2[k, top : top + part_rows, ch : 2 * ch] = shifted.reshape(part_rows, ch).astype(jnp.bfloat16)
            grads2[k, top : top + part_rows, 2 * ch : 3 * ch] = gb
            g_next[h * tall : (h + 1) * tall] = now
            gmid = dot(grads2[k, top : top + part_rows, :], wt_t[...]) * slope2[q]
            top += line
            left, right = column_shift(gmid, width, 1), column_shift(gmid, width, -1)
            grads1[k, top : top + part_rows, 0:ch] = left.astype(jnp.bfloat16)
            grads1[k, top : top + part_rows, ch : 2 * ch] = gmid.astype(jnp.bfloat16)
            grads1[k, top : top + part_rows, 2 * ch : 3 * ch] = right.astype(jnp.bfloat16)

        @pl.when(jnp.logical_not(first))
        def _():
            for h in range(CUT):
                q = CUT * k + h
                top = h * part_rows
                back = dot(grads1[k, top + 2 * line : top + 2 * line + part_rows, :], ws_t[0 : 3 * ch, :])
                back += dot(grads1[k, top + line : top + line + part_rows, :], ws_t[3 * ch : 6 * ch, :])
                back += dot(grads1[k, top : top + part_rows, :], ws_t[6 * ch : 9 * ch, :])
                gu = back * slope1[q]
                x = fwd_in[q].astype(jnp.float32)
                inv = inv_rms_of(x)
                gx = inv * gu - x * (inv * inv * inv) * jnp.mean(gu * x, axis=-1, keepdims=True)
                bwd_out[q] = (bwd_in[q].astype(jnp.float32) + gx).astype(jnp.bfloat16)
                b_copy(q).start()

        @pl.when(first & (c == 0))
        def _():
            kernel_terms(m)

    lag = chunks - 1 + 2 * (sections - 1)

    def tick(t, carry):
        i = t - sec

        @pl.when((i >= 0) & (i < total))
        def _():
            forward(i)

        @pl.when(t == jnp.where(first, sections - 1, 0))
        def _():
            for tap in range(9):
                ws_t[tap * ch : (tap + 1) * ch, :] = ws_ref[tap * ch : (tap + 1) * ch, :].T
            for tap in range(3):
                wt_t[tap * ch : (tap + 1) * ch, :] = wt_ref[tap * ch : (tap + 1) * ch, :].T

        j = t - (lag - sec)

        @pl.when((j >= 0) & (j < total))
        def _():
            backward(j)

        return carry

    lax.fori_loop(0, lag + total, tick, 0)

    @pl.when(jnp.logical_not(first))
    def _():
        def late(m, carry):
            kernel_terms(m)
            return carry

        lax.fori_loop(0, micros, late, 0)

    def piece(d):
        space = acc[pl.ds(pl.multiple_of(d * n_space, 8), n_space), :]
        time = acc[pl.ds(pl.multiple_of(9 * ch + d * n_time, 8), n_time), :]
        return jnp.concatenate([space, time], axis=0)

    def pair_copy(p):
        return pltpu.make_async_remote_copy(
            src_ref=pair_out.at[p], dst_ref=pair_in.at[p],
            send_sem=p_send.at[p], recv_sem=p_recv.at[p],
            device_id={"dp": dp + 1 - 2 * core}, device_id_type=MESH,
        )

    def chip_copy(p, slot):
        return pltpu.make_async_remote_copy(
            src_ref=chip_out.at[p], dst_ref=chip_in.at[slot],
            send_sem=c_send.at[p], recv_sem=c_recv.at[slot],
            device_id={"dp": 2 * p + core}, device_id_type=MESH,
        )

    order = [(chip + o) % chips for o in range(1, chips)]
    for p in order + [chip]:
        pair_out[p] = piece(2 * p + 1 - core).astype(jnp.bfloat16)
        pair_copy(p).start()
    for p in order:
        pair_copy(p).wait_recv()
        chip_out[p] = (piece(2 * p + core) + pair_in[p].astype(jnp.float32)).astype(jnp.bfloat16)
        chip_copy(p, chip).start()
    pair_copy(chip).wait_recv()
    share = piece(dp) + pair_in[chip].astype(jnp.float32)
    for p in order:
        chip_copy(p, p).wait_recv()
        share += chip_in[p].astype(jnp.float32)
    ds_ref[...] = grad_scale * share[:n_space]
    dt_ref[...] = grad_scale * share[n_space:]
    for p in order + [chip]:
        pair_copy(p).wait_send()
    for p in order:
        chip_copy(p, chip).wait_send()

    @pl.when(jnp.logical_not(last))
    def _():
        for k in range(CUT * total):
            f_copy(k).wait_send()

    @pl.when(jnp.logical_not(first))
    def _():
        for k in range(CUT * total):
            b_copy(k).wait_send()


def local(latents, cotangent, spatial_kernels, temporal_kernels):
    micros, crops, frames, height, width, ch = latents.shape
    sections = lax.axis_size("section")
    replicas = lax.axis_size("dp")
    chunks = frames // PER
    rows = height * PER * width
    line = PER * width
    total = micros * chunks
    vmem = pl.BlockSpec(memory_space=pltpu.VMEM)
    bf, f32 = jnp.bfloat16, jnp.float32
    chips = replicas // 2
    share = 12 * ch // replicas
    cells = micros * replicas * crops * frames * height * width
    grad_scale = 1.0 / math.sqrt(cells)
    grad_space, grad_time = pl.pallas_call(
        functools.partial(
            kernel, (micros, chunks, height, width, ch, sections, replicas, grad_scale)
        ),
        out_shape=(
            jax.ShapeDtypeStruct((9 * ch // replicas, ch), f32),
            jax.ShapeDtypeStruct((3 * ch // replicas, ch), f32),
        ),
        in_specs=[pl.BlockSpec(memory_space=pltpu.HBM)] * 4,
        out_specs=(vmem, vmem),
        scratch_shapes=[
            pltpu.VMEM((micros, frames, height, width, ch), bf),
            pltpu.VMEM((micros, frames, height, width, ch), bf),
            pltpu.VMEM((9 * ch, ch), bf),
            pltpu.VMEM((3 * ch, ch), bf),
            pltpu.VMEM((CUT * total, rows // CUT, ch), bf),
            pltpu.VMEM((CUT * total, rows // CUT, ch), bf),
            pltpu.VMEM((CUT * total, rows // CUT, ch), bf),
            pltpu.VMEM((CUT * total, rows // CUT, ch), bf),
            pltpu.VMEM((CUT * total, rows // CUT, ch), f32),
            pltpu.VMEM((CUT * total, rows // CUT, ch), f32),
            pltpu.VMEM((total, ch, rows), bf),
            pltpu.VMEM((total, ch, rows), bf),
            pltpu.VMEM((9 * ch, ch), bf),
            pltpu.VMEM((3 * ch, ch), bf),
            pltpu.VMEM((rows + 2 * line, 3 * ch), bf),
            pltpu.VMEM((rows, 3 * ch), bf),
            pltpu.VMEM((total, rows + 2 * line, 3 * ch), bf),
            pltpu.VMEM((total, rows, 3 * ch), bf),
            pltpu.VMEM((height, PER, width, ch), f32),
            pltpu.VMEM((height, PER, width, ch), f32),
            pltpu.VMEM((height, PER, width, ch), f32),
            pltpu.VMEM((12 * ch, ch), f32),
            pltpu.VMEM((chips, share, ch), bf),
            pltpu.VMEM((chips, share, ch), bf),
            pltpu.VMEM((chips, share, ch), bf),
            pltpu.VMEM((chips, share, ch), bf),
            pltpu.SemaphoreType.DMA((4,)),
            pltpu.SemaphoreType.DMA((CUT * total,)),
            pltpu.SemaphoreType.DMA((CUT * total,)),
            pltpu.SemaphoreType.DMA((CUT * total,)),
            pltpu.SemaphoreType.DMA((CUT * total,)),
            pltpu.SemaphoreType.DMA((chips,)),
            pltpu.SemaphoreType.DMA((chips,)),
            pltpu.SemaphoreType.DMA((chips,)),
            pltpu.SemaphoreType.DMA((chips,)),
        ],
        compiler_params=pltpu.CompilerParams(
            collective_id=0, has_side_effects=True, vmem_limit_bytes=62 * 1024 * 1024
        ),
    )(latents[:, 0], cotangent[:, 0], spatial_kernels[0], temporal_kernels[0])
    return (grad_space[None], grad_time[None])


def solution(mesh):
    in_specs = (
        P(None, "dp", None, None, None, None),
        P(None, "dp", None, None, None, None),
        P("section", None, None),
        P("section", None, None),
    )
    out_specs = (P("section", "dp", None), P("section", "dp", None))
    return jax.shard_map(local, mesh=mesh, in_specs=in_specs, out_specs=out_specs, check_vma=False)
```
